256 devices in a mesh: store: 32 (over z, y), head: 8 (over x, core).
Axes of the slice: x: 4, y: 4, z: 8, core: 2. Of those that a mesh axis runs over, the one named last changes fastest.
Arguments:
- queries: bfloat16 [32768, 4096], P('store', 'head'), may hold values from -7.2 to 7.2
- neighbour_ids: int32 [512, 2], P('store'), may hold values from 0 to 255, as said below
- neighbour_kv: bfloat16 [256, 128, 2, 4096], P('store', None, None, 'head'), may hold values from -7.2 to 7.2
- out_weight: bfloat16 [4096, 8192], P('head'), may hold values from -0.375 to 0.375
Outputs:
- mixed: bfloat16 [32768, 8192], P('store', 'head')
The draws below stay inside these ranges and needn't reach their ends.
Inputs may be any that keep to these rules, and one draw needn't show every extreme that they name: `neighbour_ids`: the two neighbours of a segment differ. The 32 ids of the segments of one index of store (aligned blocks of 16 rows) are all different, and at most 2 of them lie in the ids of one holder (ids h * 8 to h * 8 + 7); every such block reaches 2 for some holder.
All inputs are finite; a program needn't handle non-finite values.
Results may differ from the reference program's by a relative error of at most 0.0159.
Values may be sent and summed in bfloat16 or wider, within the bound.
No kernel may reach another device: no remote copies, remote signals or barrier semaphores. Data moves between devices by JAX's collectives and lax.ppermute only.
A program may use at most 128 MiB of HBM per device.

```python
import jax
import jax.numpy as jnp
from jax import lax

D = 8192
DH = 128
HEADS = 32
SEG = 64
NB_LEN = 128
SEG_DEV = 16
NB_DEV = 8
TOKENS = 32768
NEIGH = 256
CAP = 2
N_STORE = 32
N_HEAD = 8


def draw_neighbour_kv(key, part):
    key = jax.random.fold_in(key, 11)
    key_base = jax.random.fold_in(key, 0)
    base = jax.random.truncated_normal(key_base, -6.0, 6.0, (NEIGH, NB_LEN, 2, HEADS * DH)) * 1.2
    return base.astype(jnp.bfloat16)


def draw_queries(key, part):
    key = jax.random.fold_in(key, 23)
    key_base = jax.random.fold_in(key, 0)
    base = jax.random.truncated_normal(key_base, -6.0, 6.0, (TOKENS, HEADS * DH)) * 1.2
    return base.astype(jnp.bfloat16)


def draw_neighbour_ids(key, part):
    key = jax.random.fold_in(key, 37)
    subkeys = jax.random.split(key, 6)
    holders = NEIGH // NB_DEV
    refs_per = 2 * SEG_DEV
    popularity = jax.random.randint(subkeys[0], (holders,), 0, 3) * 300
    busiest = jax.random.randint(subkeys[1], (), 0, holders)
    preference = popularity + jnp.where(jnp.arange(holders) == busiest, 100000, 0)
    jitter = jax.random.randint(subkeys[2], (holders, holders, CAP), 0, 1000)
    flat_score = (jitter + preference[None, :, None]).reshape(holders, holders * CAP)
    ranking = flat_score * (holders * CAP) + jnp.arange(holders * CAP)[None, :]
    chosen = lax.top_k(ranking, refs_per)[1]
    holder = chosen // CAP
    rank_index = chosen % CAP
    hot_start = jax.random.randint(subkeys[3], (holders, holders), 0, 2) == 0
    offset_base = jnp.where(hot_start, 0, jax.random.randint(subkeys[4], (holders, holders), 0, NB_DEV))
    start_pick = jnp.take_along_axis(offset_base, holder, axis=1)
    neighbour = holder * NB_DEV + (start_pick + rank_index) % NB_DEV
    shuffle = jnp.argsort(jax.random.randint(subkeys[5], (holders, refs_per), 0, 1 << 20) * refs_per + jnp.arange(refs_per)[None, :], axis=1)
    neighbour = jnp.take_along_axis(neighbour, shuffle, axis=1)
    return neighbour.reshape(holders * SEG_DEV, 2).astype(jnp.int32)


def level_of(own_key, dims, pieces, smallest, largest):
    factor_of, own = 1.0, jax.random.fold_in(own_key, 6)
    for axis_at, parts in pieces:
        heights = jnp.exp(jax.random.uniform(jax.random.fold_in(own, axis_at), (parts,), jnp.float32, smallest / len(pieces), largest / len(pieces)))
        factor_of = factor_of * jnp.repeat(heights, dims[axis_at] // parts).reshape([-1 if axis == axis_at else 1 for axis in range(len(dims))])
    return factor_of


def scatter_about(stream_key, dims, width, bound, pieces=(), held_as=jnp.bfloat16):
    drawn = jax.random.normal(stream_key, dims, jnp.float32) * width
    if len(pieces) > 0:
        drawn = level_of(stream_key, dims, pieces, -0.22, 0.18) * drawn
    return jnp.clip(drawn, min=-bound, max=bound).astype(held_as)


def setup_inputs(seed: int = 0) -> dict:
    splits = jax.random.split(jax.random.key(seed), 5)
    return {
        "queries": draw_queries(jax.random.fold_in(splits[4], 71), 0),
        "neighbour_ids": draw_neighbour_ids(jax.random.fold_in(splits[4], 71), 0),
        "neighbour_kv": draw_neighbour_kv(jax.random.fold_in(splits[4], 71), 0),
        "out_weight": scatter_about(splits[3], (HEADS * DH, D), (HEADS * DH // 16) ** -0.5, 0.375, ((0, 8),)),
    }


def reference(queries, neighbour_ids, neighbour_kv, out_weight):
    score_scale = DH ** -0.5
    group_cols = HEADS * DH // N_HEAD
    block_queries = queries.reshape(N_STORE, SEG_DEV * SEG, HEADS * DH)
    block_refs = neighbour_ids.reshape(N_STORE, SEG_DEV * 2)
    group_weights = out_weight.reshape(N_HEAD, group_cols, D)

    def one_block(block_pair):
        block_rows, block_ids = block_pair
        picked = neighbour_kv[block_ids].reshape(SEG_DEV, 2, NB_LEN, 2, HEADS, DH).astype(jnp.float32)
        query_f32 = block_rows.reshape(SEG_DEV, SEG, HEADS, DH).astype(jnp.float32)
        scores = jnp.einsum("cqhd,cjkhd->chqjk", query_f32, picked[:, :, :, 0], precision=lax.Precision.HIGHEST) * score_scale
        part_max = jnp.max(scores, axis=-1)
        weights = jnp.exp(scores - part_max[..., None])
        part_total = jnp.sum(weights, axis=-1)
        rounded = lax.optimization_barrier(weights.astype(jnp.bfloat16)).astype(jnp.float32)
        part_sum = jnp.einsum("chqjk,cjkhd->chqjd", rounded, picked[:, :, :, 1], precision=lax.Precision.HIGHEST)
        row_max = jnp.max(part_max, axis=-1, keepdims=True)
        factor = jnp.exp(part_max - row_max)
        merged_sum = jnp.sum(part_sum * factor[..., None], axis=3)
        merged_total = jnp.sum(part_total * factor, axis=-1)
        context = jnp.transpose(merged_sum / merged_total[..., None], (0, 2, 1, 3))
        context = context.reshape(SEG_DEV * SEG, N_HEAD, group_cols).astype(jnp.bfloat16)

        def add_group(running, group_pair):
            group_context, group_weight = group_pair
            group_term = jnp.dot(group_context, group_weight, preferred_element_type=jnp.float32).astype(jnp.bfloat16)
            group_term = lax.optimization_barrier(group_term)
            return running + group_term.astype(jnp.float32), None

        running, _ = lax.scan(add_group, jnp.zeros((SEG_DEV * SEG, D), jnp.float32), (jnp.transpose(context, (1, 0, 2)), group_weights))
        return running.astype(jnp.bfloat16)

    blocks = lax.map(one_block, (block_queries, block_refs))
    return blocks.reshape(N_STORE * SEG_DEV * SEG, D)
```

```python
import functools

import jax
import jax.numpy as jnp
import numpy as np
from jax import lax
from jax.experimental import pallas as pl
from jax.experimental.pallas import tpu as pltpu
from jax.sharding import Mesh, PartitionSpec as P

NZ, NY, NX, NC = 8, 4, 4, 2
DH = 128
SEG = 64
SEGS = 16
REFS = 2 * SEGS
NB_DEV = 8
NB_LEN = 128
ROW_NB = NY * NB_DEV
SLOTS = 8
TILES = SLOTS // 2
OUT_ROWS = TILES * DH + 16
MB = 1 << 20


def attn_kernel(ids_ref, me_ref, q_ref, kv_ref, out_ref, slot_ref):
    zi = pl.program_id(0)
    zme = me_ref[0]
    count = jnp.int32(0)
    for i in range(REFS):
        slot_ref[i] = jnp.int32(0)
    for i in range(REFS):
        hit = ids_ref[zi * REFS + i] // ROW_NB == zme
        slot_ref[count] = jnp.int32(i)
        count = count + hit.astype(jnp.int32)
    low = lax.broadcasted_iota(jnp.int32, (1, 2 * SEG), 1) < SEG
    his, mids, los = [], [], []
    for t in range(TILES):
        queries, keys, values = [], [], []
        for half in range(2):
            ref = slot_ref[2 * t + half]
            nb = ids_ref[zi * REFS + ref] % ROW_NB
            start = pl.multiple_of((ref // 2) * SEG, SEG)
            queries.append(q_ref[pl.ds(start, SEG), :])
            yi, at = nb // NB_DEV, nb % NB_DEV
            keys.append(kv_ref[yi, 0, 0, at])
            values.append(kv_ref[yi, 0, 1, at])
        pair = jnp.concatenate(queries, axis=0)
        nt = (((1,), (1,)), ((), ()))
        s0 = lax.dot_general(keys[0], pair, nt, preferred_element_type=jnp.float32)
        s1 = lax.dot_general(keys[1], pair, nt, preferred_element_type=jnp.float32)
        scores = jnp.where(low, s0, s1) * (DH**-0.5)
        top = jnp.max(scores, axis=0, keepdims=True)
        weights = jnp.exp(scores - top)
        total = jnp.sum(weights, axis=0, keepdims=True)
        rounded = weights.astype(jnp.bfloat16)
        o0 = jnp.dot(values[0], rounded, preferred_element_type=jnp.float32)
        o1 = jnp.dot(values[1], rounded, preferred_element_type=jnp.float32)
        out = jnp.where(low, o0, o1) * (1.0 / total)
        out_ref[0, t * DH : (t + 1) * DH, :] = out.astype(jnp.bfloat16)
        lse = top + jnp.log(total)
        hi = lse.astype(jnp.bfloat16).astype(jnp.float32)
        mid = (lse - hi).astype(jnp.bfloat16).astype(jnp.float32)
        his.append(hi)
        mids.append(mid)
        los.append(lse - hi - mid)
    tail = jnp.concatenate(his + mids + los + [jnp.zeros((4, 2 * SEG), jnp.float32)], axis=0)
    out_ref[0, TILES * DH :, :] = tail.astype(jnp.bfloat16)


def attend(ids_all, zme, q_all, kv_all, hh):
    return pl.pallas_call(
        attn_kernel,
        grid_spec=pltpu.PrefetchScalarGridSpec(
            num_scalar_prefetch=2,
            grid=(NZ,),
            in_specs=[
                pl.BlockSpec((SEGS * SEG, DH), lambda z, *_: (z, hh)),
                pl.BlockSpec(
                    (NY, 1, 2, NB_DEV, DH, DH), lambda z, *_: (0, hh, 0, 0, 0, 0)
                ),
            ],
            out_specs=pl.BlockSpec((1, OUT_ROWS, 2 * SEG), lambda z, *_: (z, 0, 0)),
            scratch_shapes=[pltpu.SMEM((2 * REFS,), jnp.int32)],
        ),
        out_shape=jax.ShapeDtypeStruct((NZ, OUT_ROWS, 2 * SEG), jnp.bfloat16),
        compiler_params=pltpu.CompilerParams(vmem_limit_bytes=24 * MB),
        cost_estimate=pl.CostEstimate(
            flops=32 * 4 * 2 * DH**3 * 4, bytes_accessed=8 * MB, transcendentals=32 * DH * DH
        ),
        name="attend",
    )(ids_all, zme, q_all, kv_all)


def merge_kernel(ids_ref, part_ref, out_ref, lse_ref, place_ref, count_ref):
    for z in range(NZ):
        count_ref[z] = jnp.int32(0)
        tail = part_ref[z, TILES * DH :, :].astype(jnp.float32)
        lse_ref[z] = tail[0:4] + tail[4:8] + tail[8:12]
    for i in range(REFS):
        row = ids_ref[i] // ROW_NB
        rank = count_ref[row]
        count_ref[row] = rank + 1
        place_ref[i] = row * SLOTS + rank
    low = lax.broadcasted_iota(jnp.int32, (1, 2 * SEG), 1) < SEG
    for p in range(SEGS // 2):
        sums, lses = [], []
        for j in range(2):
            halves_o, halves_l = [], []
            for side in range(2):
                place = place_ref[2 * (2 * p + side) + j]
                z, rank = place // SLOTS, place % SLOTS
                tile, half = rank // 2, rank % 2
                start = pl.multiple_of(tile * DH, DH)
                part = part_ref[z, pl.ds(start, DH), :].astype(jnp.float32)
                lse = lse_ref[z, pl.ds(tile, 1), :]
                shift = jnp.where(half == side, 0, SEG)
                halves_o.append(pltpu.roll(part, shift, 1))
                halves_l.append(pltpu.roll(lse, shift, 1))
            sums.append(jnp.where(low, halves_o[0], halves_o[1]))
            lses.append(jnp.where(low, halves_l[0], halves_l[1]))
        top = jnp.maximum(lses[0], lses[1])
        f0, f1 = jnp.exp(lses[0] - top), jnp.exp(lses[1] - top)
        scale = 1.0 / (f0 + f1)
        context = ((f0 * scale) * sums[0] + (f1 * scale) * sums[1]).astype(jnp.bfloat16)
        for x in range(NX):
            out_ref[x, :, p * 2 * SEG : (p + 1) * 2 * SEG] = context


def merge(ids, parts):
    return pl.pallas_call(
        merge_kernel,
        grid_spec=pltpu.PrefetchScalarGridSpec(
            num_scalar_prefetch=1,
            grid=(),
            in_specs=[pl.BlockSpec(memory_space=pltpu.VMEM)],
            out_specs=pl.BlockSpec(memory_space=pltpu.VMEM),
            scratch_shapes=[
                pltpu.VMEM((NZ, TILES, 2 * SEG), jnp.float32),
                pltpu.SMEM((REFS,), jnp.int32),
                pltpu.SMEM((NZ,), jnp.int32),
            ],
        ),
        out_shape=jax.ShapeDtypeStruct((NX, DH, SEGS * SEG), jnp.bfloat16),
        compiler_params=pltpu.CompilerParams(vmem_limit_bytes=24 * MB),
        cost_estimate=pl.CostEstimate(
            flops=4 * DH * SEGS * SEG, bytes_accessed=3 * MB, transcendentals=2 * SEGS * SEG
        ),
        name="merge",
    )(ids, parts)


def body(queries, neighbour_ids, neighbour_kv, out_weight):
    heads = queries.shape[1] // DH
    zme = lax.axis_index("z").astype(jnp.int32).reshape(1)
    cme = lax.axis_index("core")
    ids = neighbour_ids.reshape(-1)
    ids_all = lax.all_gather(ids, "z", tiled=True)
    cols = out_weight.shape[1] // (NX * NC)

    def both(value):
        return jnp.broadcast_to(value[None], (NY, *value.shape))

    q_all, kv_all = [], []
    for pair in range(heads // 2):
        at = slice(pair * 2 * DH, (pair + 1) * 2 * DH)
        q_all.append(lax.all_gather(queries[:, at], "z", tiled=True))
    for pair in range(heads // 2):
        at = slice(pair * 2 * DH, (pair + 1) * 2 * DH)
        block = neighbour_kv[:, :, :, at].reshape(NB_DEV, NB_LEN, 2, 2, DH)
        keys = jnp.transpose(block[:, :, 0], (2, 0, 1, 3))
        values = jnp.transpose(block[:, :, 1], (2, 0, 3, 1))
        own = jnp.stack([keys, values], axis=1)
        kv_all.append(lax.all_to_all(both(own), "y", 0, 0, tiled=True))
    shares = jnp.transpose(out_weight.reshape(-1, NX, NC * cols), (1, 0, 2))
    plane = lax.all_to_all(shares, "x", 0, 0, tiled=True)
    plane = plane.reshape(NX, -1, NC, cols)
    w_own = lax.dynamic_index_in_dim(plane, cme, 2, keepdims=False)
    w_send = lax.dynamic_index_in_dim(plane, 1 - cme, 2, keepdims=False)
    swap = [(0, 1), (1, 0)]
    w_other = lax.ppermute(w_send, "core", swap)

    contract = (((0,), (0,)), ((), ()))
    total = None
    for head in range(heads):
        parts = attend(ids_all, zme, q_all[head // 2], kv_all[head // 2], head % 2)
        back = lax.all_to_all(parts, "z", 0, 0, tiled=True)
        context = merge(ids, back)
        gathered = lax.all_to_all(context, "x", 0, 0, tiled=True)
        other = lax.ppermute(gathered, "core", swap)
        rows = slice(head * DH, (head + 1) * DH)
        for ctx, weight in ((gathered, w_own), (other, w_other)):
            term = lax.dot_general(
                ctx.reshape(NX * DH, -1),
                weight[:, rows].reshape(NX * DH, cols),
                contract,
                preferred_element_type=jnp.float32,
            )
            total = term if total is None else total + term
    return total.astype(jnp.bfloat16)


def solution(mesh):
    fine = Mesh(np.asarray(mesh.devices).reshape(NZ, NY, NX, NC), ("z", "y", "x", "core"))
    store, head = ("z", "y"), ("x", "core")
    in_specs = (
        P(store, head),
        P(store, None),
        P(store, None, None, head),
        P(head, None),
    )
    return jax.shard_map(
        body, mesh=fine, in_specs=in_specs, out_specs=P(store, head), check_vma=False
    )
```

```python
import jax
import jax.numpy as jnp
import numpy as np
from jax import lax
from jax.experimental import pallas as pl
from jax.experimental.pallas import tpu as pltpu
from jax.sharding import Mesh, PartitionSpec as P

NZ, NY, NX, NC = 8, 4, 4, 2
DH = 128
SEG = 64
SEGS = 16
ROWS = SEG * SEGS
REFS = 2 * SEGS
NB_DEV = 8
NB_LEN = 128
NB_BITS = 3
CAP = 2
PAIR = CAP * SEG
TAIL = 32
PART = NZ * DH + TAIL
MB = 1 << 20


def attn_kernel(plan_ref, *refs):
    q_refs, (kv_ref, out_ref, lse_ref) = refs[:NY], refs[NY:]
    zi = pl.program_id(0)
    yme = plan_ref[NZ * NY * CAP]
    low = lax.broadcasted_iota(jnp.int32, (1, PAIR), 1) < SEG
    nt = (((1,), (1,)), ((), ()))
    scores, values = [], []
    for a in range(NY):
        queries, keys = [], []
        for r in range(CAP):
            code = plan_ref[(zi * NY + a) * CAP + r]
            at = code & (NB_DEV - 1)
            start = pl.multiple_of((code >> NB_BITS) * SEG, SEG)
            queries.append(q_refs[a][pl.ds(start, SEG), :])
            keys.append(kv_ref[0, at])
            values.append(kv_ref[1, at])
        values[-2:] = [jnp.concatenate(values[-2:], axis=0)]
        pair = jnp.concatenate(queries, axis=0)
        keys = jnp.concatenate(keys, axis=0)
        both = lax.dot_general(keys, pair, nt, preferred_element_type=jnp.float32)
        scores.append(jnp.where(low, both[:NB_LEN], both[NB_LEN:]))
    scores = jnp.concatenate(scores, axis=1) * (DH**-0.5)
    top = jnp.max(scores, axis=0, keepdims=True)
    weights = jnp.exp(scores - top)
    total = jnp.sum(weights, axis=0, keepdims=True)
    rounded = weights.astype(jnp.bfloat16)
    inverse = 1.0 / total
    lse = top + jnp.log(total)
    hi = lse.astype(jnp.bfloat16).astype(jnp.float32)
    mid = (lse - hi).astype(jnp.bfloat16).astype(jnp.float32)
    lo = lse - hi - mid
    start = pl.multiple_of(zi * DH, DH)
    for a in range(NY):
        at = slice(a * PAIR, (a + 1) * PAIR)
        both = jnp.dot(values[a], rounded[:, at], preferred_element_type=jnp.float32)
        out = (jnp.where(low, both[:DH], both[DH:]) * inverse[:, at]).astype(jnp.bfloat16)
        out_ref[(yme + a) & (NY - 1), pl.ds(start, DH), :] = out
        for k, piece in enumerate((hi, mid, lo)):
            lse_ref[a, pl.ds(k * NZ + zi, 1), :] = piece[:, at]

    @pl.when(zi == NZ - 1)
    def _():
        for a in range(NY):
            lse_ref[a, 3 * NZ :, :] = jnp.zeros((TAIL - 3 * NZ, PAIR), jnp.float32)
            tail = lse_ref[a].astype(jnp.bfloat16)
            out_ref[(yme + a) & (NY - 1), NZ * DH :, :] = tail


def attend(plan, q_blocks, kv, head, at):
    sq = pl.Squeezed()
    return pl.pallas_call(
        attn_kernel,
        grid_spec=pltpu.PrefetchScalarGridSpec(
            num_scalar_prefetch=1,
            grid=(NZ,),
            in_specs=[pl.BlockSpec((ROWS, DH), lambda z, *_: (0, head))] * NY
            + [pl.BlockSpec((sq, sq, 2, NB_DEV, DH, DH), lambda z, *_: (z, at, 0, 0, 0, 0))],
            out_specs=pl.BlockSpec((NY, PART, PAIR), lambda z, *_: (0, 0, 0)),
            scratch_shapes=[pltpu.VMEM((NY, TAIL, PAIR), jnp.float32)],
        ),
        out_shape=jax.ShapeDtypeStruct((NY, PART, PAIR), jnp.bfloat16),
        compiler_params=pltpu.CompilerParams(vmem_limit_bytes=48 * MB),
        cost_estimate=pl.CostEstimate(
            flops=32 * 4 * 2 * DH**3 * 4, bytes_accessed=20 * MB, transcendentals=32 * DH * DH
        ),
        name="attend",
    )(plan, *q_blocks, kv)


def merge_kernel(place_ref, part_ref, out_ref, lse_ref):
    for y in range(NY):
        tail = part_ref[y, NZ * DH :, :].astype(jnp.float32)
        lse_ref[y] = tail[0:NZ] + tail[NZ : 2 * NZ] + tail[2 * NZ : 3 * NZ]
    low = lax.broadcasted_iota(jnp.int32, (1, PAIR), 1) < SEG
    for p in range(SEGS // 2):
        sums, lses = [], []
        for j in range(2):
            halves_o, halves_l = [], []
            for side in range(2):
                code = place_ref[2 * (2 * p + side) + j]
                half, y, z = code & 1, (code >> 1) & (NY - 1), code >> 3
                start = pl.multiple_of(z * DH, DH)
                part = part_ref[y, pl.ds(start, DH), :].astype(jnp.float32)
                lse = lse_ref[y, pl.ds(z, 1), :]
                shift = jnp.where(half == side, 0, SEG)
                halves_o.append(pltpu.roll(part, shift, 1))
                halves_l.append(pltpu.roll(lse, shift, 1))
            sums.append(jnp.where(low, halves_o[0], halves_o[1]))
            lses.append(jnp.where(low, halves_l[0], halves_l[1]))
        top = jnp.maximum(lses[0], lses[1])
        f0, f1 = jnp.exp(lses[0] - top), jnp.exp(lses[1] - top)
        scale = 1.0 / (f0 + f1)
        context = (f0 * scale) * sums[0] + (f1 * scale) * sums[1]
        out_ref[p * PAIR : (p + 1) * PAIR, :] = jnp.transpose(context).astype(jnp.bfloat16)


def merge(place, parts):
    return pl.pallas_call(
        merge_kernel,
        grid_spec=pltpu.PrefetchScalarGridSpec(
            num_scalar_prefetch=1,
            grid=(),
            in_specs=[pl.BlockSpec(memory_space=pltpu.VMEM)],
            out_specs=pl.BlockSpec(memory_space=pltpu.VMEM),
            scratch_shapes=[pltpu.VMEM((NY, NZ, PAIR), jnp.float32)],
        ),
        out_shape=jax.ShapeDtypeStruct((ROWS, DH), jnp.bfloat16),
        compiler_params=pltpu.CompilerParams(vmem_limit_bytes=16 * MB),
        cost_estimate=pl.CostEstimate(
            flops=8 * DH * ROWS, bytes_accessed=8 * MB, transcendentals=2 * ROWS
        ),
        name="merge",
    )(place, parts)


def project(contexts, weights, head, total, last):
    groups = len(contexts)
    cols = weights[0].shape[1]
    width = 256
    first = total is None

    def kernel(*refs):
        ctx, wgt = refs[:groups], refs[groups : 2 * groups]
        out_ref = refs[-1]
        left = jnp.concatenate([ref[...] for ref in ctx], axis=1)
        right = jnp.concatenate([ref[...] for ref in wgt], axis=0)
        term = jnp.dot(left, right, preferred_element_type=jnp.float32)
        if not first:
            term = term + refs[2 * groups][...]
        out_ref[...] = term.astype(out_ref.dtype)

    block = pl.BlockSpec((ROWS, width), lambda n: (0, n))
    in_specs = [pl.BlockSpec((ROWS, DH), lambda n: (0, 0))] * groups
    in_specs += [pl.BlockSpec((DH, width), lambda n: (head, n))] * groups
    operands = [*contexts, *weights]
    if not first:
        in_specs.append(block)
        operands.append(total)
    return pl.pallas_call(
        kernel,
        grid=(cols // width,),
        in_specs=in_specs,
        out_specs=block,
        out_shape=jax.ShapeDtypeStruct((ROWS, cols), jnp.bfloat16 if last else jnp.float32),
        input_output_aliases={} if first or last else {2 * groups: 0},
        compiler_params=pltpu.CompilerParams(vmem_limit_bytes=16 * MB),
        cost_estimate=pl.CostEstimate(
            flops=2 * ROWS * cols * groups * DH, bytes_accessed=12 * MB, transcendentals=0
        ),
        name="project",
    )(*operands)


def ring(axis, size, step):
    return [(i, (i + step) % size) for i in range(size)]


def earlier_equal(keys):
    order = jnp.arange(keys.shape[-1])
    same = keys[..., :, None] == keys[..., None, :]
    return jnp.sum((same & (order[None, :] < order[:, None])).astype(jnp.int32), axis=-1)


def body(queries, neighbour_ids, neighbour_kv, out_weight):
    heads = queries.shape[1] // DH
    yme, xme, cme = (lax.axis_index(a).astype(jnp.int32) for a in ("y", "x", "core"))
    cols = out_weight.shape[1] // (NX * NC)
    barrier = lax.optimization_barrier

    split = heads - 1
    block = neighbour_kv.reshape(NB_DEV, NB_LEN, 2, heads, DH)
    keys = jnp.transpose(block[:, :, 0], (2, 0, 1, 3))
    values = jnp.transpose(block[:, :, 1], (2, 0, 3, 1))
    own = jnp.stack([keys, values], axis=1)
    kv_first = lax.all_gather(own[:split], "z")
    kv_last = lax.all_gather(own[split:], "z")

    chip_cols = NC * cols
    shares = []
    for dx in range(NX):
        target = (xme + dx) % NX
        share = lax.dynamic_slice_in_dim(out_weight, target * chip_cols, chip_cols, 1)
        shares.append(lax.ppermute(share, "x", ring("x", NX, dx)) if dx else share)

    q_all = [queries] + [lax.ppermute(queries, "y", ring("y", NY, -d)) for d in range(1, NY)]

    ids = neighbour_ids.reshape(-1)
    ids_row = lax.all_gather(ids, "y")
    asked = jnp.roll(ids_row, -yme, axis=0)
    holder = asked >> NB_BITS
    rank = earlier_equal(holder)
    want = (jnp.arange(NZ) * NY + yme)[:, None, None, None]
    hit = (holder[None, :, None, :] == want) & (
        rank[None, :, None, :] == jnp.arange(CAP)[None, None, :, None]
    )
    code = (jnp.arange(REFS) // 2) * NB_DEV + (asked & (NB_DEV - 1))
    plan = jnp.sum(jnp.where(hit, code[None, :, None, :], 0), axis=-1).reshape(-1)
    plan = jnp.concatenate([plan, yme.reshape(1)])
    mine = ids >> NB_BITS
    place = mine * CAP + earlier_equal(mine)

    swap = [(0, 1), (1, 0)]
    weights = []
    for share in shares:
        keep = lax.dynamic_slice_in_dim(share, cme * cols, cols, 1)
        rest = lax.dynamic_slice_in_dim(share, (1 - cme) * cols, cols, 1)
        weights += [keep, lax.ppermute(rest, "core", swap)]

    kv_first, q_all, weights, plan, place = barrier((kv_first, q_all, weights, plan, place))

    def near(context):
        return [context] + [lax.ppermute(context, "x", ring("x", NX, d)) for d in range(1, NX)]

    def both_cores(came):
        return [c for own in came for c in (own, lax.ppermute(own, "core", swap))]

    def after(value, *others):
        return barrier((value, others))[0]

    def send(parts):
        return lax.all_to_all(parts, "y", 0, 0, tiled=True)

    parts0 = attend(plan, q_all, kv_first, 0, 0)
    back0 = send(parts0)
    parts1 = attend(plan, q_all, kv_first, 1, 1)
    back1 = send(parts1)
    parts2 = attend(after(plan, parts1), q_all, kv_first, 2, 2)
    context0 = merge(place, after(back0, parts2))
    came0 = near(context0)
    back2 = send(after(parts2, came0))
    context1 = merge(place, after(back1, came0))
    came1 = near(context1)
    parts3 = attend(plan, q_all, after(kv_last, context1), 3, 0)
    back3 = send(after(parts3, came1))
    full0 = both_cores(came0)
    context2 = merge(place, after(back2, parts3))
    came2 = near(context2)
    total = project(after(full0, context2), weights, 0, None, False)
    total = project(both_cores(came1), weights, 1, total, False)
    context3 = merge(place, after(back3, came2, total))
    came3 = near(context3)
    total = project(both_cores(after(came2, context3)), weights, 2, total, False)
    came3[1:] = after(came3[1:], total)
    return project(both_cores(came3), weights, 3, total, True)


def solution(mesh):
    fine = Mesh(np.asarray(mesh.devices).reshape(NZ, NY, NX, NC), ("z", "y", "x", "core"))
    store, head = ("z", "y"), ("x", "core")
    in_specs = (
        P(store, head),
        P(store, None),
        P(store, None, None, head),
        P(head, None),
    )
    return jax.shard_map(
        body, mesh=fine, in_specs=in_specs, out_specs=P(store, head), check_vma=False
    )
```

```python
import functools

import jax
import jax.numpy as jnp
import numpy as np
from jax import lax
from jax.experimental import pallas as pl
from jax.experimental.pallas import tpu as pltpu
from jax.sharding import Mesh, PartitionSpec as P

NZ, NY, NX, NC = 8, 4, 4, 2
DH = 128
SEG = 64
SEGS = 16
ROWS = SEG * SEGS
REFS = 2 * SEGS
NB_DEV = 8
NB_LEN = 128
NB_BITS = 3
CAP = 2
PAIR = CAP * SEG
TAIL = 32
PART = NZ * DH + TAIL
MB = 1 << 20


def near_kernel(plan_ref, *refs):
    q_refs, kv_refs, (kv_ref, sem), rest = refs[:NY], refs[NY : NY + NZ + 1], refs[-2:], refs[NY + NZ + 1 : -2]
    zi = pl.program_id(0)
    half = NZ // 2

    @pl.when(zi == 0)
    def _():
        for r in range(NZ + 1):
            to = r if r <= half else r - 1
            dst = kv_ref.at[to]
            if r in (half, half + 1):
                dst = kv_ref.at[to, pl.ds(r - half, 1)]
            pltpu.make_async_copy(kv_refs[r], dst, sem.at[to]).start()

    pltpu.make_async_copy(kv_refs[0], kv_ref.at[zi], sem.at[zi]).wait()
    attn_kernel(True, plan_ref, *q_refs, kv_ref.at[zi], *rest)


def attn_kernel(apart, plan_ref, *refs):
    q_refs, kv_ref, out_refs, lse_ref = refs[:NY], refs[NY], refs[NY + 1 : -1], refs[-1]
    zi = pl.program_id(0)
    yme = plan_ref[NZ * NY * CAP]
    place = (zi + plan_ref[NZ * NY * CAP + 1]) & (NZ - 1)
    if apart:
        outs = out_refs
    else:
        outs = [out_refs[0].at[(yme + a) & (NY - 1)] for a in range(NY)]
    low = lax.broadcasted_iota(jnp.int32, (1, PAIR), 1) < SEG
    nt = (((1,), (1,)), ((), ()))
    scores, values = [], []
    for a in range(NY):
        queries, keys = [], []
        for r in range(CAP):
            code = plan_ref[(zi * NY + a) * CAP + r]
            at = code & (NB_DEV - 1)
            start = pl.multiple_of((code >> NB_BITS) * SEG, SEG)
            queries.append(q_refs[a][pl.ds(start, SEG), :])
            keys.append(kv_ref[0, at])
            values.append(kv_ref[1, at])
        values[-2:] = [jnp.concatenate(values[-2:], axis=0)]
        pair = jnp.concatenate(queries, axis=0)
        keys = jnp.concatenate(keys, axis=0)
        both = lax.dot_general(keys, pair, nt, preferred_element_type=jnp.float32)
        scores.append(jnp.where(low, both[:NB_LEN], both[NB_LEN:]))
    scores = jnp.concatenate(scores, axis=1) * (DH**-0.5)
    top = jnp.max(scores, axis=0, keepdims=True)
    weights = jnp.exp(scores - top)
    total = jnp.sum(weights, axis=0, keepdims=True)
    rounded = weights.astype(jnp.bfloat16)
    inverse = 1.0 / total
    lse = top + jnp.log(total)
    hi = lse.astype(jnp.bfloat16).astype(jnp.float32)
    mid = (lse - hi).astype(jnp.bfloat16).astype(jnp.float32)
    lo = lse - hi - mid
    start = pl.multiple_of(place * DH, DH)
    for a in range(NY):
        at = slice(a * PAIR, (a + 1) * PAIR)
        both = jnp.dot(values[a], rounded[:, at], preferred_element_type=jnp.float32)
        out = (jnp.where(low, both[:DH], both[DH:]) * inverse[:, at]).astype(jnp.bfloat16)
        outs[a][pl.ds(start, DH), :] = out
        for k, piece in enumerate((hi, mid, lo)):
            lse_ref[a, pl.ds(k * NZ + place, 1), :] = piece[:, at]

    @pl.when(zi == NZ - 1)
    def _():
        for a in range(NY):
            lse_ref[a, 3 * NZ :, :] = jnp.zeros((TAIL - 3 * NZ, PAIR), jnp.float32)
            tail = lse_ref[a].astype(jnp.bfloat16)
            outs[a][NZ * DH :, :] = tail


def attend(plan, q_blocks, kv, head, at):
    sq = pl.Squeezed()
    near = isinstance(kv, list)
    lse = [pltpu.VMEM((NY, TAIL, PAIR), jnp.float32)]
    if near:
        kernel, operands = near_kernel, kv
        kv_specs = [pl.BlockSpec(memory_space=pl.ANY)] * len(kv)
        out_specs = [pl.BlockSpec((PART, PAIR), lambda z, *_: (0, 0))] * NY
        out_shape = [jax.ShapeDtypeStruct((PART, PAIR), jnp.bfloat16)] * NY
        scratch = lse + [
            pltpu.VMEM((NZ, 2, NB_DEV, DH, DH), jnp.bfloat16),
            pltpu.SemaphoreType.DMA((NZ,)),
        ]
    else:
        kernel, operands = functools.partial(attn_kernel, False), [kv]
        kv_specs = [pl.BlockSpec((sq, sq, 2, NB_DEV, DH, DH), lambda z, *_: (z, at, 0, 0, 0, 0))]
        out_specs = pl.BlockSpec((NY, PART, PAIR), lambda z, *_: (0, 0, 0))
        out_shape = jax.ShapeDtypeStruct((NY, PART, PAIR), jnp.bfloat16)
        scratch = lse
    return pl.pallas_call(
        kernel,
        grid_spec=pltpu.PrefetchScalarGridSpec(
            num_scalar_prefetch=1,
            grid=(NZ,),
            in_specs=[pl.BlockSpec((ROWS, DH), lambda z, *_: (0, head))] * NY + kv_specs,
            out_specs=out_specs,
            scratch_shapes=scratch,
        ),
        out_shape=out_shape,
        compiler_params=pltpu.CompilerParams(vmem_limit_bytes=60 * MB),
        cost_estimate=pl.CostEstimate(
            flops=32 * 4 * 2 * DH**3 * 4, bytes_accessed=20 * MB, transcendentals=32 * DH * DH
        ),
        name="attend",
    )(plan, *q_blocks, *operands)


def merge_kernel(counts, place_ref, *refs):
    part_refs, (out_ref, lse_ref, near_ref) = refs[: sum(counts)], refs[sum(counts) :]
    low = lax.broadcasted_iota(jnp.int32, (1, PAIR), 1) < SEG
    for head, count in enumerate(counts):
        head_refs, part_refs = part_refs[:count], part_refs[count:]
        if count > 1:
            part_ref = near_ref
            for y in range(NY):
                near_ref[y] = head_refs[y][...]
        else:
            part_ref = head_refs[0]
        for y in range(NY):
            tail = part_ref[y, NZ * DH :, :].astype(jnp.float32)
            lse_ref[y] = tail[0:NZ] + tail[NZ : 2 * NZ] + tail[2 * NZ : 3 * NZ]
        for p in range(SEGS // 2):
            sums, lses = [], []
            for j in range(2):
                halves_o, halves_l = [], []
                for side in range(2):
                    code = place_ref[2 * (2 * p + side) + j + (REFS if count > 1 else 0)]
                    half, y, z = code & 1, (code >> 1) & (NY - 1), code >> 3
                    start = pl.multiple_of(z * DH, DH)
                    part = part_ref[y, pl.ds(start, DH), :].astype(jnp.float32)
                    lse = lse_ref[y, pl.ds(z, 1), :]
                    shift = jnp.where(half == side, 0, SEG)
                    halves_o.append(pltpu.roll(part, shift, 1))
                    halves_l.append(pltpu.roll(lse, shift, 1))
                sums.append(jnp.where(low, halves_o[0], halves_o[1]))
                lses.append(jnp.where(low, halves_l[0], halves_l[1]))
            top = jnp.maximum(lses[0], lses[1])
            f0, f1 = jnp.exp(lses[0] - top), jnp.exp(lses[1] - top)
            scale = 1.0 / (f0 + f1)
            context = (f0 * scale) * sums[0] + (f1 * scale) * sums[1]
            out_ref[p * PAIR : (p + 1) * PAIR, head * DH : (head + 1) * DH] = jnp.transpose(
                context
            ).astype(jnp.bfloat16)


def merge(place, *heads):
    counts = [len(parts) for parts in heads]
    near_shape = (NY, PART, PAIR) if max(counts) > 1 else (1, 16, PAIR)
    return pl.pallas_call(
        functools.partial(merge_kernel, counts),
        grid_spec=pltpu.PrefetchScalarGridSpec(
            num_scalar_prefetch=1,
            grid=(),
            in_specs=[pl.BlockSpec(memory_space=pltpu.VMEM)] * sum(counts),
            out_specs=pl.BlockSpec(memory_space=pltpu.VMEM),
            scratch_shapes=[
                pltpu.VMEM((NY, NZ, PAIR), jnp.float32),
                pltpu.VMEM(near_shape, jnp.bfloat16),
            ],
        ),
        out_shape=jax.ShapeDtypeStruct((ROWS, len(heads) * DH), jnp.bfloat16),
        compiler_params=pltpu.CompilerParams(vmem_limit_bytes=16 * MB),
        cost_estimate=pl.CostEstimate(
            flops=8 * DH * ROWS, bytes_accessed=8 * MB, transcendentals=2 * ROWS
        ),
        name="merge",
    )(place, *[part for parts in heads for part in parts])


def project(where, spread, shares, other, total, last):
    cols = other.shape[2]
    width = 256
    first = total is None
    sq = pl.Squeezed()
    groups = len(spread) * NX * NC

    def kernel(_, *refs):
        ctx, wgt = refs[:groups], refs[groups : 2 * groups]
        out_ref = refs[-1]
        left = jnp.concatenate([ref[...] for ref in ctx], axis=1)
        right = jnp.concatenate([ref[...] for ref in wgt], axis=0)
        term = jnp.dot(left, right, preferred_element_type=jnp.float32)
        if not first:
            term = term + refs[2 * groups][...]
        out_ref[...] = term.astype(out_ref.dtype)

    def own_rows(head, d):
        at_x = (lambda at: at[0] * NC) if d == 0 else (lambda at: 0)
        return lambda n, at: (head, (at_x(at) + at[1]) * (cols // width) + n)

    def other_rows(head, d):
        return lambda n, *_: (d, head, n)

    block = pl.BlockSpec((ROWS, width), lambda n, *_: (0, n))
    in_specs = [pl.BlockSpec((ROWS, DH), lambda n, *_: (0, 0))] * groups
    operands = [context for _, contexts in spread for context in contexts]
    for head, _ in spread:
        for d in range(NX):
            in_specs += [
                pl.BlockSpec((DH, width), own_rows(head, d)),
                pl.BlockSpec((sq, DH, width), other_rows(head, d)),
            ]
            operands += [shares[d], other]
    if not first:
        in_specs.append(block)
        operands.append(total)
    return pl.pallas_call(
        kernel,
        grid_spec=pltpu.PrefetchScalarGridSpec(
            num_scalar_prefetch=1, grid=(cols // width,), in_specs=in_specs, out_specs=block
        ),
        out_shape=jax.ShapeDtypeStruct((ROWS, cols), jnp.bfloat16 if last else jnp.float32),
        input_output_aliases={} if first or last else {2 * groups + 1: 0},
        compiler_params=pltpu.CompilerParams(vmem_limit_bytes=(16 if last else 48) * MB),
        cost_estimate=pl.CostEstimate(
            flops=2 * ROWS * cols * groups * DH, bytes_accessed=12 * MB, transcendentals=0
        ),
        name="project",
    )(where, *operands)


def ring(axis, size, step):
    return [(i, (i + step) % size) for i in range(size)]


def earlier_equal(keys):
    order = jnp.arange(keys.shape[-1])
    same = keys[..., :, None] == keys[..., None, :]
    return jnp.sum((same & (order[None, :] < order[:, None])).astype(jnp.int32), axis=-1)


def body(queries, neighbour_ids, neighbour_kv, out_weight):
    heads = queries.shape[1] // DH
    zme, yme, xme, cme = (lax.axis_index(a).astype(jnp.int32) for a in ("z", "y", "x", "core"))
    cols = out_weight.shape[1] // (NX * NC)
    barrier = lax.optimization_barrier

    def after(value, *others):
        return barrier((value, others))[0]

    block = neighbour_kv.reshape(NB_DEV, NB_LEN, 2, heads, DH)
    keys = jnp.transpose(block[:, :, 0], (2, 0, 1, 3))
    values = jnp.transpose(block[:, :, 1], (2, 0, 3, 1))
    own = jnp.stack([keys, values], axis=1)
    kv_mid = lax.all_gather(own[1:3], "z")
    kv_last = lax.all_gather(own[3:], "z")

    def up(value):
        return lax.ppermute(value, "z", ring("z", NZ, 1))

    def down(value):
        return lax.ppermute(value, "z", ring("z", NZ, -1))

    below, above = [own[0]], [own[0]]
    for _ in range(NZ // 2 - 1):
        below.append(up(below[-1]))
        above.append(down(above[-1]))
    kv_near = above + [up(below[-1][:1]), down(above[-1][1:])] + below[:0:-1]

    chip_cols = NC * cols
    shares = [out_weight]
    for d in range(1, NX):
        target = (xme + d) % NX
        share = lax.dynamic_slice_in_dim(out_weight, target * chip_cols, chip_cols, 1)
        shares.append(lax.ppermute(share, "x", ring("x", NX, d)))

    ids = neighbour_ids.reshape(-1)
    width = queries.shape[1]
    id_rows = jnp.pad(ids.astype(queries.dtype).reshape(1, REFS), ((0, 15), (0, width - REFS)))
    asker = jnp.concatenate([queries, id_rows], axis=0)
    q_all = [asker] + [lax.ppermute(asker, "y", ring("y", NY, -d)) for d in range(1, NY)]
    asked = jnp.stack([q[ROWS, :REFS] for q in q_all]).astype(jnp.int32)

    holder = asked >> NB_BITS
    rank = earlier_equal(holder)
    want = (jnp.arange(NZ) * NY + yme)[:, None, None, None]
    hit = (holder[None, :, None, :] == want) & (
        rank[None, :, None, :] == jnp.arange(CAP)[None, None, :, None]
    )
    code = (jnp.arange(REFS) // 2) * NB_DEV + (asked & (NB_DEV - 1))
    plan = jnp.sum(jnp.where(hit, code[None, :, None, :], 0), axis=-1)
    plan_near = jnp.concatenate([jnp.roll(plan, -zme, axis=0).reshape(-1), yme[None], zme[None]])
    plan = jnp.concatenate([plan.reshape(-1), yme[None], jnp.zeros((1,), jnp.int32)])
    mine = ids >> NB_BITS
    near_mine = (mine // NY) * NY + ((yme - mine) & (NY - 1))
    place = jnp.concatenate([mine, near_mine]) * CAP + jnp.tile(earlier_equal(mine), 2)

    swap = [(0, 1), (1, 0)]

    def near(context):
        return [context] + [lax.ppermute(context, "x", ring("x", NX, d)) for d in range(1, NX)]

    def both_cores(came):
        return [c for own in came for c in (own, lax.ppermute(own, "core", swap))]

    def send(parts):
        return lax.all_to_all(parts, "y", 0, 0, tiled=True)

    parts0 = attend(plan_near, q_all, kv_near, 0, 0)
    back0 = [lax.ppermute(p, "y", ring("y", NY, d)) if d else p for d, p in enumerate(parts0)]
    came0 = near(merge(place, back0))

    parts1 = attend(plan, q_all, after(kv_mid, back0), 1, 0)
    back1 = send(parts1)
    parts2 = attend(plan, q_all, kv_mid, 2, 1)

    shares = after(after(shares, back0), parts1)
    first_col = [xme * chip_cols] + [0] * (NX - 1)
    rest = [
        lax.dynamic_slice_in_dim(share, at + (1 - cme) * cols, cols, 1)
        for share, at in zip(shares, first_col)
    ]
    other = lax.ppermute(jnp.stack(rest), "core", swap)
    where = jnp.stack([xme, cme])

    back2 = send(after(parts2, came0))
    context1 = merge(place, [after(back1, parts2)])
    came1 = near(context1)
    parts3 = attend(plan, q_all, after(kv_last, context1), 3, 0)
    back3 = send(after(parts3, came1))
    context2 = merge(place, [after(back2, parts3)])
    came2 = near(context2)
    spread = [(0, both_cores(after(came0, context2))), (1, both_cores(came1))]
    total = project(where, spread, shares, other, None, False)
    context3 = merge(place, [after(back3, came2, total)])
    came3 = near(context3)
    spread = [(2, both_cores(after(came2, context3)))]
    total = project(where, spread, shares, other, total, False)
    came3[1:] = after(came3[1:], total)
    return project(where, [(3, both_cores(came3))], shares, other, total, True)


def solution(mesh):
    fine = Mesh(np.asarray(mesh.devices).reshape(NZ, NY, NX, NC), ("z", "y", "x", "core"))
    store, head = ("z", "y"), ("x", "core")
    in_specs = (
        P(store, head),
        P(store, None),
        P(store, None, None, head),
        P(head, None),
    )
    return jax.shard_map(
        body, mesh=fine, in_specs=in_specs, out_specs=P(store, head), check_vma=False
    )
```

```python
import functools

import jax
import jax.numpy as jnp
import numpy as np
from jax import lax
from jax.experimental import pallas as pl
from jax.experimental.pallas import tpu as pltpu
from jax.sharding import Mesh, PartitionSpec as P

NZ, NY, NX, NC = 8, 4, 4, 2
DH = 128
SEG = 64
SEGS = 16
ROWS = SEG * SEGS
REFS = 2 * SEGS
NB_DEV = 8
NB_LEN = 128
NB_BITS = 3
CAP = 2
PAIR = CAP * SEG
TAIL = 32
PART = NZ * DH + TAIL
MB = 1 << 20


def near_kernel(plan_ref, *refs):
    q_refs, kv_refs, (kv_ref, sem), rest = refs[:NY], refs[NY : NY + NZ + 1], refs[-2:], refs[NY + NZ + 1 : -2]
    zi = pl.program_id(0)
    half = NZ // 2

    @pl.when(zi == 0)
    def _():
        for r in range(NZ + 1):
            to = r if r <= half else r - 1
            dst = kv_ref.at[to]
            if r in (half, half + 1):
                dst = kv_ref.at[to, pl.ds(r - half, 1)]
            pltpu.make_async_copy(kv_refs[r], dst, sem.at[to]).start()

    pltpu.make_async_copy(kv_refs[0], kv_ref.at[zi], sem.at[zi]).wait()
    attn_kernel(True, plan_ref, *q_refs, kv_ref.at[zi], *rest)


def attn_kernel(apart, plan_ref, *refs):
    q_refs, kv_ref, out_refs, lse_ref = refs[:NY], refs[NY], refs[NY + 1 : -1], refs[-1]
    zi = pl.program_id(0)
    yme = plan_ref[NZ * NY * CAP]
    place = (zi + plan_ref[NZ * NY * CAP + 1]) & (NZ - 1)
    if apart:
        outs = out_refs
    else:
        outs = [out_refs[0].at[(yme + a) & (NY - 1)] for a in range(NY)]
    low = lax.broadcasted_iota(jnp.int32, (1, PAIR), 1) < SEG
    nt = (((1,), (1,)), ((), ()))
    scores, values = [], []
    for a in range(NY):
        queries, keys = [], []
        for r in range(CAP):
            code = plan_ref[(zi * NY + a) * CAP + r]
            at = code & (NB_DEV - 1)
            start = pl.multiple_of((code >> NB_BITS) * SEG, SEG)
            queries.append(q_refs[a][pl.ds(start, SEG), :])
            keys.append(kv_ref[0, at])
            values.append(kv_ref[1, at])
        values[-2:] = [jnp.concatenate(values[-2:], axis=0)]
        pair = jnp.concatenate(queries, axis=0)
        keys = jnp.concatenate(keys, axis=0)
        both = lax.dot_general(keys, pair, nt, preferred_element_type=jnp.float32)
        scores.append(jnp.where(low, both[:NB_LEN], both[NB_LEN:]))
    scores = jnp.concatenate(scores, axis=1) * (DH**-0.5)
    top = jnp.max(scores, axis=0, keepdims=True)
    weights = jnp.exp(scores - top)
    total = jnp.sum(weights, axis=0, keepdims=True)
    rounded = weights.astype(jnp.bfloat16)
    inverse = 1.0 / total
    lse = top + jnp.log(total)
    hi = lse.astype(jnp.bfloat16).astype(jnp.float32)
    mid = (lse - hi).astype(jnp.bfloat16).astype(jnp.float32)
    lo = lse - hi - mid
    start = pl.multiple_of(place * DH, DH)
    for a in range(NY):
        at = slice(a * PAIR, (a + 1) * PAIR)
        both = jnp.dot(values[a], rounded[:, at], preferred_element_type=jnp.float32)
        out = (jnp.where(low, both[:DH], both[DH:]) * inverse[:, at]).astype(jnp.bfloat16)
        outs[a][pl.ds(start, DH), :] = out
        for k, piece in enumerate((hi, mid, lo)):
            lse_ref[a, pl.ds(k * NZ + place, 1), :] = piece[:, at]

    @pl.when(zi == NZ - 1)
    def _():
        for a in range(NY):
            lse_ref[a, 3 * NZ :, :] = jnp.zeros((TAIL - 3 * NZ, PAIR), jnp.float32)
            tail = lse_ref[a].astype(jnp.bfloat16)
            outs[a][NZ * DH :, :] = tail


def attend(plan, q_blocks, kv, head, at):
    sq = pl.Squeezed()
    near = isinstance(kv, list)
    lse = [pltpu.VMEM((NY, TAIL, PAIR), jnp.float32)]
    if near:
        kernel, operands = near_kernel, kv
        kv_specs = [pl.BlockSpec(memory_space=pl.ANY)] * len(kv)
        out_specs = [pl.BlockSpec((PART, PAIR), lambda z, *_: (0, 0))] * NY
        out_shape = [jax.ShapeDtypeStruct((PART, PAIR), jnp.bfloat16)] * NY
        scratch = lse + [
            pltpu.VMEM((NZ, 2, NB_DEV, DH, DH), jnp.bfloat16),
            pltpu.SemaphoreType.DMA((NZ,)),
        ]
    else:
        kernel, operands = functools.partial(attn_kernel, False), [kv]
        kv_specs = [pl.BlockSpec((sq, sq, 2, NB_DEV, DH, DH), lambda z, *_: (z, at, 0, 0, 0, 0))]
        out_specs = pl.BlockSpec((NY, PART, PAIR), lambda z, *_: (0, 0, 0))
        out_shape = jax.ShapeDtypeStruct((NY, PART, PAIR), jnp.bfloat16)
        scratch = lse
    return pl.pallas_call(
        kernel,
        grid_spec=pltpu.PrefetchScalarGridSpec(
            num_scalar_prefetch=1,
            grid=(NZ,),
            in_specs=[pl.BlockSpec((ROWS, DH), lambda z, *_: (0, head))] * NY + kv_specs,
            out_specs=out_specs,
            scratch_shapes=scratch,
        ),
        out_shape=out_shape,
        compiler_params=pltpu.CompilerParams(vmem_limit_bytes=60 * MB),
        cost_estimate=pl.CostEstimate(
            flops=32 * 4 * 2 * DH**3 * 4, bytes_accessed=20 * MB, transcendentals=32 * DH * DH
        ),
        name="attend",
    )(plan, *q_blocks, *operands)


def merge_kernel(counts, place_ref, *refs):
    part_refs, (out_ref, lse_ref, near_ref) = refs[: sum(counts)], refs[sum(counts) :]
    low = lax.broadcasted_iota(jnp.int32, (1, PAIR), 1) < SEG
    for head, count in enumerate(counts):
        head_refs, part_refs = part_refs[:count], part_refs[count:]
        if count > 1:
            part_ref = near_ref
            for y in range(NY):
                near_ref[y] = head_refs[y][...]
        else:
            part_ref = head_refs[0]
        for y in range(NY):
            tail = part_ref[y, NZ * DH :, :].astype(jnp.float32)
            lse_ref[y] = tail[0:NZ] + tail[NZ : 2 * NZ] + tail[2 * NZ : 3 * NZ]
        for p in range(SEGS // 2):
            sums, lses = [], []
            for j in range(2):
                halves_o, halves_l = [], []
                for side in range(2):
                    code = place_ref[2 * (2 * p + side) + j + (REFS if count > 1 else 0)]
                    half, y, z = code & 1, (code >> 1) & (NY - 1), code >> 3
                    start = pl.multiple_of(z * DH, DH)
                    part = part_ref[y, pl.ds(start, DH), :].astype(jnp.float32)
                    lse = lse_ref[y, pl.ds(z, 1), :]
                    shift = jnp.where(half == side, 0, SEG)
                    halves_o.append(pltpu.roll(part, shift, 1))
                    halves_l.append(pltpu.roll(lse, shift, 1))
                sums.append(jnp.where(low, halves_o[0], halves_o[1]))
                lses.append(jnp.where(low, halves_l[0], halves_l[1]))
            top = jnp.maximum(lses[0], lses[1])
            f0, f1 = jnp.exp(lses[0] - top), jnp.exp(lses[1] - top)
            scale = 1.0 / (f0 + f1)
            context = (f0 * scale) * sums[0] + (f1 * scale) * sums[1]
            out_ref[p * PAIR : (p + 1) * PAIR, head * DH : (head + 1) * DH] = jnp.transpose(
                context
            ).astype(jnp.bfloat16)


def merge(place, *heads):
    counts = [len(parts) for parts in heads]
    near_shape = (NY, PART, PAIR) if max(counts) > 1 else (1, 16, PAIR)
    return pl.pallas_call(
        functools.partial(merge_kernel, counts),
        grid_spec=pltpu.PrefetchScalarGridSpec(
            num_scalar_prefetch=1,
            grid=(),
            in_specs=[pl.BlockSpec(memory_space=pltpu.VMEM)] * sum(counts),
            out_specs=pl.BlockSpec(memory_space=pltpu.VMEM),
            scratch_shapes=[
                pltpu.VMEM((NY, NZ, PAIR), jnp.float32),
                pltpu.VMEM(near_shape, jnp.bfloat16),
            ],
        ),
        out_shape=jax.ShapeDtypeStruct((ROWS, len(heads) * DH), jnp.bfloat16),
        compiler_params=pltpu.CompilerParams(vmem_limit_bytes=16 * MB),
        cost_estimate=pl.CostEstimate(
            flops=8 * DH * ROWS, bytes_accessed=8 * MB, transcendentals=2 * ROWS
        ),
        name="merge",
    )(place, *[part for parts in heads for part in parts])


def project(where, spread, shares, other, total, last):
    cols = other.shape[2]
    width = 512
    first = total is None
    sq = pl.Squeezed()
    groups = len(spread) * NX * NC

    def kernel(_, *refs):
        ctx, wgt = refs[:groups], refs[groups : 2 * groups]
        out_ref = refs[-1]
        left = jnp.concatenate([ref[...] for ref in ctx], axis=1)
        right = jnp.concatenate([ref[...] for ref in wgt], axis=0)
        term = jnp.dot(left, right, preferred_element_type=jnp.float32)
        if not first:
            term = term + refs[2 * groups][...]
        out_ref[...] = term.astype(out_ref.dtype)

    def own_rows(head, d):
        at_x = (lambda at: at[0] * NC) if d == 0 else (lambda at: 0)
        return lambda n, at: (head, (at_x(at) + at[1]) * (cols // width) + n)

    def other_rows(head, d):
        return lambda n, *_: (d, head, n)

    block = pl.BlockSpec((ROWS, width), lambda n, *_: (0, n))
    in_specs = [pl.BlockSpec((ROWS, DH), lambda n, *_: (0, 0))] * groups
    operands = [context for _, contexts in spread for context in contexts]
    for head, _ in spread:
        for d in range(NX):
            in_specs += [
                pl.BlockSpec((DH, width), own_rows(head, d)),
                pl.BlockSpec((sq, DH, width), other_rows(head, d)),
            ]
            operands += [shares[d], other]
    if not first:
        in_specs.append(block)
        operands.append(total)
    return pl.pallas_call(
        kernel,
        grid_spec=pltpu.PrefetchScalarGridSpec(
            num_scalar_prefetch=1, grid=(cols // width,), in_specs=in_specs, out_specs=block
        ),
        out_shape=jax.ShapeDtypeStruct((ROWS, cols), jnp.bfloat16 if last else jnp.float32),
        input_output_aliases={} if first or last else {2 * groups + 1: 0},
        compiler_params=pltpu.CompilerParams(vmem_limit_bytes=60 * MB),
        cost_estimate=pl.CostEstimate(
            flops=2 * ROWS * cols * groups * DH, bytes_accessed=12 * MB, transcendentals=0
        ),
        name="project",
    )(where, *operands)


def ring(axis, size, step):
    return [(i, (i + step) % size) for i in range(size)]


def earlier_equal(keys):
    order = jnp.arange(keys.shape[-1])
    same = keys[..., :, None] == keys[..., None, :]
    return jnp.sum((same & (order[None, :] < order[:, None])).astype(jnp.int32), axis=-1)


def body(queries, neighbour_ids, neighbour_kv, out_weight):
    heads = queries.shape[1] // DH
    zme, yme, xme, cme = (lax.axis_index(a).astype(jnp.int32) for a in ("z", "y", "x", "core"))
    cols = out_weight.shape[1] // (NX * NC)
    barrier = lax.optimization_barrier

    def after(value, *others):
        return barrier((value, others))[0]

    block = neighbour_kv.reshape(NB_DEV, NB_LEN, 2, heads, DH)
    keys = jnp.transpose(block[:, :, 0], (2, 0, 1, 3))
    values = jnp.transpose(block[:, :, 1], (2, 0, 3, 1))
    own = jnp.stack([keys, values], axis=1)
    kv_mid = lax.all_gather(own[1:3], "z")
    kv_last = lax.all_gather(own[3:], "z")

    def up(value):
        return lax.ppermute(value, "z", ring("z", NZ, 1))

    def down(value):
        return lax.ppermute(value, "z", ring("z", NZ, -1))

    below, above = [own[0]], [own[0]]
    for _ in range(NZ // 2 - 1):
        below.append(up(below[-1]))
        above.append(down(above[-1]))
    kv_near = above + [up(below[-1][:1]), down(above[-1][1:])] + below[:0:-1]

    chip_cols = NC * cols
    shares = [out_weight]
    for d in range(1, NX):
        target = (xme + d) % NX
        share = lax.dynamic_slice_in_dim(out_weight, target * chip_cols, chip_cols, 1)
        shares.append(lax.ppermute(share, "x", ring("x", NX, d)))

    ids = neighbour_ids.reshape(-1)
    width = queries.shape[1]
    id_rows = jnp.pad(ids.astype(queries.dtype).reshape(1, REFS), ((0, 15), (0, width - REFS)))
    asker = jnp.concatenate([queries, id_rows], axis=0)
    q_all = [asker] + [lax.ppermute(asker, "y", ring("y", NY, -d)) for d in range(1, NY)]
    asked = jnp.stack([q[ROWS, :REFS] for q in q_all]).astype(jnp.int32)

    holder = asked >> NB_BITS
    rank = earlier_equal(holder)
    want = (jnp.arange(NZ) * NY + yme)[:, None, None, None]
    hit = (holder[None, :, None, :] == want) & (
        rank[None, :, None, :] == jnp.arange(CAP)[None, None, :, None]
    )
    code = (jnp.arange(REFS) // 2) * NB_DEV + (asked & (NB_DEV - 1))
    plan = jnp.sum(jnp.where(hit, code[None, :, None, :], 0), axis=-1)
    plan_near = jnp.concatenate([jnp.roll(plan, -zme, axis=0).reshape(-1), yme[None], zme[None]])
    plan = jnp.concatenate([plan.reshape(-1), yme[None], jnp.zeros((1,), jnp.int32)])
    mine = ids >> NB_BITS
    near_mine = (mine // NY) * NY + ((yme - mine) & (NY - 1))
    place = jnp.concatenate([mine, near_mine]) * CAP + jnp.tile(earlier_equal(mine), 2)

    swap = [(0, 1), (1, 0)]

    def near(context):
        return [context] + [lax.ppermute(context, "x", ring("x", NX, d)) for d in range(1, NX)]

    def both_cores(came):
        return [c for own in came for c in (own, lax.ppermute(own, "core", swap))]

    def send(parts):
        return lax.all_to_all(parts, "y", 0, 0, tiled=True)

    parts0 = attend(plan_near, q_all, kv_near, 0, 0)
    back0 = [lax.ppermute(p, "y", ring("y", NY, d)) if d else p for d, p in enumerate(parts0)]
    came0 = near(merge(place, back0))

    parts1 = attend(plan, q_all, after(kv_mid, back0), 1, 0)
    back1 = send(parts1)
    parts2 = attend(plan, q_all, kv_mid, 2, 1)

    shares = after(after(shares, back0), parts1)
    first_col = [xme * chip_cols] + [0] * (NX - 1)
    rest = [
        lax.dynamic_slice_in_dim(share, at + (1 - cme) * cols, cols, 1)
        for share, at in zip(shares, first_col)
    ]
    other = lax.ppermute(jnp.stack(rest), "core", swap)
    where = jnp.stack([xme, cme])

    back2 = send(after(parts2, came0))
    context1 = merge(place, [after(back1, parts2)])
    came1 = near(context1)
    parts3 = attend(plan, q_all, after(kv_last, context1), 3, 0)
    back3 = send(after(parts3, came1))
    context2 = merge(place, [after(back2, parts3)])
    came2 = near(context2)
    spread = [(0, both_cores(after(came0, context2))), (1, both_cores(came1))]
    total = project(where, spread, shares, other, None, False)
    context3 = merge(place, [after(back3, came2, total)])
    came3 = near(context3)
    spread = [(2, both_cores(after(came2, context3)))]
    total = project(where, spread, shares, other, total, False)
    came3[1:] = after(came3[1:], total)
    return project(where, [(3, both_cores(came3))], shares, other, total, True)


def solution(mesh):
    fine = Mesh(np.asarray(mesh.devices).reshape(NZ, NY, NX, NC), ("z", "y", "x", "core"))
    store, head = ("z", "y"), ("x", "core")
    in_specs = (
        P(store, head),
        P(store, None),
        P(store, None, None, head),
        P(head, None),
    )
    return jax.shard_map(
        body, mesh=fine, in_specs=in_specs, out_specs=P(store, head), check_vma=False
    )
```

```python
import functools

import jax
import jax.numpy as jnp
import numpy as np
from jax import lax
from jax.experimental import pallas as pl
from jax.experimental.pallas import tpu as pltpu
from jax.sharding import Mesh, PartitionSpec as P

NZ, NY, NX, NC = 8, 4, 4, 2
DH = 128
SEG = 64
SEGS = 16
ROWS = SEG * SEGS
REFS = 2 * SEGS
NB_DEV = 8
NB_LEN = 128
NB_BITS = 3
CAP = 2
PAIR = CAP * SEG
TAIL = 32
PART = NZ * DH + TAIL
MB = 1 << 20


def near_kernel(plan_ref, *refs):
    q_refs, kv_refs, (kv_ref, sem), rest = refs[:NY], refs[NY : NY + NZ + 1], refs[-2:], refs[NY + NZ + 1 : -2]
    zi = pl.program_id(0)
    half = NZ // 2

    @pl.when(zi == 0)
    def _():
        for r in range(NZ + 1):
            to = r if r <= half else r - 1
            dst = kv_ref.at[to]
            if r in (half, half + 1):
                dst = kv_ref.at[to, pl.ds(r - half, 1)]
            pltpu.make_async_copy(kv_refs[r], dst, sem.at[to]).start()

    pltpu.make_async_copy(kv_refs[0], kv_ref.at[zi], sem.at[zi]).wait()
    attn_kernel(True, plan_ref, *q_refs, kv_ref.at[zi], *rest)


def attn_kernel(apart, plan_ref, *refs):
    q_refs, kv_ref, out_refs, lse_ref = refs[:NY], refs[NY], refs[NY + 1 : -1], refs[-1]
    zi = pl.program_id(0)
    yme = plan_ref[NZ * NY * CAP]
    place = (zi + plan_ref[NZ * NY * CAP + 1]) & (NZ - 1)
    if apart:
        outs = out_refs
    else:
        outs = [out_refs[0].at[(yme + a) & (NY - 1)] for a in range(NY)]
    low = lax.broadcasted_iota(jnp.int32, (1, PAIR), 1) < SEG
    nt = (((1,), (1,)), ((), ()))
    scores, values = [], []
    for a in range(NY):
        queries, keys = [], []
        for r in range(CAP):
            code = plan_ref[(zi * NY + a) * CAP + r]
            at = code & (NB_DEV - 1)
            start = pl.multiple_of((code >> NB_BITS) * SEG, SEG)
            queries.append(q_refs[a][pl.ds(start, SEG), :])
            keys.append(kv_ref[0, at])
            values.append(kv_ref[1, at])
        values[-2:] = [jnp.concatenate(values[-2:], axis=0)]
        pair = jnp.concatenate(queries, axis=0)
        keys = jnp.concatenate(keys, axis=0)
        both = lax.dot_general(keys, pair, nt, preferred_element_type=jnp.float32)
        scores.append(jnp.where(low, both[:NB_LEN], both[NB_LEN:]))
    scores = jnp.concatenate(scores, axis=1) * (DH**-0.5)
    top = jnp.max(scores, axis=0, keepdims=True)
    weights = jnp.exp(scores - top)
    total = jnp.sum(weights, axis=0, keepdims=True)
    rounded = weights.astype(jnp.bfloat16)
    inverse = 1.0 / total
    lse = top + jnp.log(total)
    hi = lse.astype(jnp.bfloat16).astype(jnp.float32)
    mid = (lse - hi).astype(jnp.bfloat16).astype(jnp.float32)
    lo = lse - hi - mid
    start = pl.multiple_of(place * DH, DH)
    for a in range(NY):
        at = slice(a * PAIR, (a + 1) * PAIR)
        both = jnp.dot(values[a], rounded[:, at], preferred_element_type=jnp.float32)
        out = (jnp.where(low, both[:DH], both[DH:]) * inverse[:, at]).astype(jnp.bfloat16)
        outs[a][pl.ds(start, DH), :] = out
        for k, piece in enumerate((hi, mid, lo)):
            lse_ref[a, pl.ds(k * NZ + place, 1), :] = piece[:, at]

    @pl.when(zi == NZ - 1)
    def _():
        for a in range(NY):
            lse_ref[a, 3 * NZ :, :] = jnp.zeros((TAIL - 3 * NZ, PAIR), jnp.float32)
            tail = lse_ref[a].astype(jnp.bfloat16)
            outs[a][NZ * DH :, :] = tail


def attend(plan, q_blocks, kv, head, at):
    sq = pl.Squeezed()
    near = isinstance(kv, list)
    lse = [pltpu.VMEM((NY, TAIL, PAIR), jnp.float32)]
    if near:
        kernel, operands = near_kernel, kv
        kv_specs = [pl.BlockSpec(memory_space=pl.ANY)] * len(kv)
        out_specs = [pl.BlockSpec((PART, PAIR), lambda z, *_: (0, 0))] * NY
        out_shape = [jax.ShapeDtypeStruct((PART, PAIR), jnp.bfloat16)] * NY
        scratch = lse + [
            pltpu.VMEM((NZ, 2, NB_DEV, DH, DH), jnp.bfloat16),
            pltpu.SemaphoreType.DMA((NZ,)),
        ]
    else:
        kernel, operands = functools.partial(attn_kernel, False), [kv]
        kv_specs = [pl.BlockSpec((sq, sq, 2, NB_DEV, DH, DH), lambda z, *_: (z, at, 0, 0, 0, 0))]
        out_specs = pl.BlockSpec((NY, PART, PAIR), lambda z, *_: (0, 0, 0))
        out_shape = jax.ShapeDtypeStruct((NY, PART, PAIR), jnp.bfloat16)
        scratch = lse
    return pl.pallas_call(
        kernel,
        grid_spec=pltpu.PrefetchScalarGridSpec(
            num_scalar_prefetch=1,
            grid=(NZ,),
            in_specs=[pl.BlockSpec((ROWS, DH), lambda z, *_: (0, head))] * NY + kv_specs,
            out_specs=out_specs,
            scratch_shapes=scratch,
        ),
        out_shape=out_shape,
        compiler_params=pltpu.CompilerParams(vmem_limit_bytes=60 * MB),
        cost_estimate=pl.CostEstimate(
            flops=32 * 4 * 2 * DH**3 * 4, bytes_accessed=20 * MB, transcendentals=32 * DH * DH
        ),
        name="attend",
    )(plan, *q_blocks, *operands)


def merge_kernel(counts, place_ref, *refs):
    part_refs, (out_ref, lse_ref, near_ref) = refs[: sum(counts)], refs[sum(counts) :]
    low = lax.broadcasted_iota(jnp.int32, (1, PAIR), 1) < SEG
    for head, count in enumerate(counts):
        head_refs, part_refs = part_refs[:count], part_refs[count:]
        if count > 1:
            part_ref = near_ref
            for y in range(NY):
                near_ref[y] = head_refs[y][...]
        else:
            part_ref = head_refs[0]
        for y in range(NY):
            tail = part_ref[y, NZ * DH :, :].astype(jnp.float32)
            lse_ref[y] = tail[0:NZ] + tail[NZ : 2 * NZ] + tail[2 * NZ : 3 * NZ]
        for p in range(SEGS // 2):
            sums, lses = [], []
            for j in range(2):
                halves_o, halves_l = [], []
                for side in range(2):
                    code = place_ref[2 * (2 * p + side) + j + (REFS if count > 1 else 0)]
                    half, y, z = code & 1, (code >> 1) & (NY - 1), code >> 3
                    start = pl.multiple_of(z * DH, DH)
                    part = part_ref[y, pl.ds(start, DH), :].astype(jnp.float32)
                    lse = lse_ref[y, pl.ds(z, 1), :]
                    shift = jnp.where(half == side, 0, SEG)
                    halves_o.append(pltpu.roll(part, shift, 1))
                    halves_l.append(pltpu.roll(lse, shift, 1))
                sums.append(jnp.where(low, halves_o[0], halves_o[1]))
                lses.append(jnp.where(low, halves_l[0], halves_l[1]))
            top = jnp.maximum(lses[0], lses[1])
            f0, f1 = jnp.exp(lses[0] - top), jnp.exp(lses[1] - top)
            scale = 1.0 / (f0 + f1)
            context = (f0 * scale) * sums[0] + (f1 * scale) * sums[1]
            out_ref[p * PAIR : (p + 1) * PAIR, head * DH : (head + 1) * DH] = jnp.transpose(
                context
            ).astype(jnp.bfloat16)


def merge(place, *heads):
    counts = [len(parts) for parts in heads]
    near_shape = (NY, PART, PAIR) if max(counts) > 1 else (1, 16, PAIR)
    return pl.pallas_call(
        functools.partial(merge_kernel, counts),
        grid_spec=pltpu.PrefetchScalarGridSpec(
            num_scalar_prefetch=1,
            grid=(),
            in_specs=[pl.BlockSpec(memory_space=pltpu.VMEM)] * sum(counts),
            out_specs=pl.BlockSpec(memory_space=pltpu.VMEM),
            scratch_shapes=[
                pltpu.VMEM((NY, NZ, PAIR), jnp.float32),
                pltpu.VMEM(near_shape, jnp.bfloat16),
            ],
        ),
        out_shape=jax.ShapeDtypeStruct((ROWS, len(heads) * DH), jnp.bfloat16),
        compiler_params=pltpu.CompilerParams(vmem_limit_bytes=16 * MB),
        cost_estimate=pl.CostEstimate(
            flops=8 * DH * ROWS, bytes_accessed=8 * MB, transcendentals=2 * ROWS
        ),
        name="merge",
    )(place, *[part for parts in heads for part in parts])


def project(where, spread, shares, other, total, last):
    cols = other.shape[2]
    width = 512
    first = total is None
    sq = pl.Squeezed()
    groups = len(spread) * NX * NC

    def kernel(_, *refs):
        ctx, wgt = refs[:groups], refs[groups : 2 * groups]
        out_ref = refs[-1]
        left = jnp.concatenate([ref[...] for ref in ctx], axis=1)
        right = jnp.concatenate([ref[...] for ref in wgt], axis=0)
        term = jnp.dot(left, right, preferred_element_type=jnp.float32)
        if not first:
            term = term + refs[2 * groups][...]
        out_ref[...] = term.astype(out_ref.dtype)

    def own_rows(head, d):
        at_x = (lambda at: at[0] * NC) if d == 0 else (lambda at: 0)
        return lambda n, at: (head, (at_x(at) + at[1]) * (cols // width) + n)

    def other_rows(head, d):
        return lambda n, *_: (d, head, n)

    block = pl.BlockSpec((ROWS, width), lambda n, *_: (0, n))
    in_specs = [pl.BlockSpec((ROWS, DH), lambda n, *_: (0, 0))] * groups
    operands = [context for _, contexts in spread for context in contexts]
    for head, _ in spread:
        for d in range(NX):
            in_specs += [
                pl.BlockSpec((DH, width), own_rows(head, d)),
                pl.BlockSpec((sq, DH, width), other_rows(head, d)),
            ]
            operands += [shares[d], other]
    if not first:
        in_specs.append(block)
        operands.append(total)
    return pl.pallas_call(
        kernel,
        grid_spec=pltpu.PrefetchScalarGridSpec(
            num_scalar_prefetch=1, grid=(cols // width,), in_specs=in_specs, out_specs=block
        ),
        out_shape=jax.ShapeDtypeStruct((ROWS, cols), jnp.bfloat16),
        input_output_aliases={} if first or last else {2 * groups + 1: 0},
        compiler_params=pltpu.CompilerParams(vmem_limit_bytes=60 * MB),
        cost_estimate=pl.CostEstimate(
            flops=2 * ROWS * cols * groups * DH, bytes_accessed=12 * MB, transcendentals=0
        ),
        name="project",
    )(where, *operands)


def ring(axis, size, step):
    return [(i, (i + step) % size) for i in range(size)]


def earlier_equal(keys):
    order = jnp.arange(keys.shape[-1])
    same = keys[..., :, None] == keys[..., None, :]
    return jnp.sum((same & (order[None, :] < order[:, None])).astype(jnp.int32), axis=-1)


def body(queries, neighbour_ids, neighbour_kv, out_weight):
    heads = queries.shape[1] // DH
    zme, yme, xme, cme = (lax.axis_index(a).astype(jnp.int32) for a in ("z", "y", "x", "core"))
    cols = out_weight.shape[1] // (NX * NC)
    barrier = lax.optimization_barrier

    def after(value, *others):
        return barrier((value, others))[0]

    block = neighbour_kv.reshape(NB_DEV, NB_LEN, 2, heads, DH)
    keys = jnp.transpose(block[:, :, 0], (2, 0, 1, 3))
    values = jnp.transpose(block[:, :, 1], (2, 0, 3, 1))
    own = jnp.stack([keys, values], axis=1)
    kv_mid = lax.all_gather(own[1:3], "z")
    kv_last = lax.all_gather(own[3:], "z")

    def up(value):
        return lax.ppermute(value, "z", ring("z", NZ, 1))

    def down(value):
        return lax.ppermute(value, "z", ring("z", NZ, -1))

    below, above = [own[0]], [own[0]]
    for _ in range(NZ // 2 - 1):
        below.append(up(below[-1]))
        above.append(down(above[-1]))
    kv_near = above + [up(below[-1][:1]), down(above[-1][1:])] + below[:0:-1]

    chip_cols = NC * cols
    shares = [out_weight]
    for d in range(1, NX):
        target = (xme + d) % NX
        share = lax.dynamic_slice_in_dim(out_weight, target * chip_cols, chip_cols, 1)
        shares.append(lax.ppermute(share, "x", ring("x", NX, d)))

    ids = neighbour_ids.reshape(-1)
    width = queries.shape[1]
    id_rows = jnp.pad(ids.astype(queries.dtype).reshape(1, REFS), ((0, 15), (0, width - REFS)))
    asker = jnp.concatenate([queries, id_rows], axis=0)
    q_all = [asker] + [lax.ppermute(asker, "y", ring("y", NY, -d)) for d in range(1, NY)]
    asked = jnp.stack([q[ROWS, :REFS] for q in q_all]).astype(jnp.int32)

    holder = asked >> NB_BITS
    rank = earlier_equal(holder)
    want = (jnp.arange(NZ) * NY + yme)[:, None, None, None]
    hit = (holder[None, :, None, :] == want) & (
        rank[None, :, None, :] == jnp.arange(CAP)[None, None, :, None]
    )
    code = (jnp.arange(REFS) // 2) * NB_DEV + (asked & (NB_DEV - 1))
    plan = jnp.sum(jnp.where(hit, code[None, :, None, :], 0), axis=-1)
    plan_near = jnp.concatenate([jnp.roll(plan, -zme, axis=0).reshape(-1), yme[None], zme[None]])
    plan = jnp.concatenate([plan.reshape(-1), yme[None], jnp.zeros((1,), jnp.int32)])
    mine = ids >> NB_BITS
    near_mine = (mine // NY) * NY + ((yme - mine) & (NY - 1))
    place = jnp.concatenate([mine, near_mine]) * CAP + jnp.tile(earlier_equal(mine), 2)

    swap = [(0, 1), (1, 0)]

    def near(context):
        return [context] + [lax.ppermute(context, "x", ring("x", NX, d)) for d in range(1, NX)]

    def both_cores(came):
        return [c for own in came for c in (own, lax.ppermute(own, "core", swap))]

    def send(parts):
        return lax.all_to_all(parts, "y", 0, 0, tiled=True)

    parts0 = attend(plan_near, q_all, kv_near, 0, 0)
    back0 = [lax.ppermute(p, "y", ring("y", NY, d)) if d else p for d, p in enumerate(parts0)]
    came0 = near(merge(place, back0))

    parts1 = attend(plan, q_all, after(kv_mid, back0), 1, 0)
    back1 = send(parts1)
    parts2 = attend(plan, q_all, kv_mid, 2, 1)

    shares = after(after(shares, back0), parts1)
    first_col = [xme * chip_cols] + [0] * (NX - 1)
    rest = [
        lax.dynamic_slice_in_dim(share, at + (1 - cme) * cols, cols, 1)
        for share, at in zip(shares, first_col)
    ]
    other = lax.ppermute(jnp.stack(rest), "core", swap)
    where = jnp.stack([xme, cme])

    back2 = send(after(parts2, came0))
    context1 = merge(place, [after(back1, parts2)])
    came1 = near(context1)
    parts3 = attend(plan, q_all, after(kv_last, context1), 3, 0)
    back3 = send(after(parts3, came1))
    context2 = merge(place, [after(back2, parts3)])
    came2 = near(context2)
    spread = [(0, both_cores(after(came0, context2))), (1, both_cores(came1))]
    total = project(where, spread, shares, other, None, False)
    context3 = merge(place, [after(back3, total)])
    came3 = near(after(context3, came2))
    spread = [(2, both_cores(after(came2, context3)))]
    total = project(where, spread, shares, other, total, False)
    came3[1:] = after(came3[1:], total)
    return project(where, [(3, both_cores(came3))], shares, other, total, True)


def solution(mesh):
    fine = Mesh(np.asarray(mesh.devices).reshape(NZ, NY, NX, NC), ("z", "y", "x", "core"))
    store, head = ("z", "y"), ("x", "core")
    in_specs = (
        P(store, head),
        P(store, None),
        P(store, None, None, head),
        P(head, None),
    )
    return jax.shard_map(
        body, mesh=fine, in_specs=in_specs, out_specs=P(store, head), check_vma=False
    )
```

```python
import functools

import jax
import jax.numpy as jnp
import numpy as np
from jax import lax
from jax.experimental import pallas as pl
from jax.experimental.pallas import tpu as pltpu
from jax.sharding import Mesh, PartitionSpec as P

NZ, NY, NX, NC = 8, 4, 4, 2
DH = 128
SEG = 64
SEGS = 16
ROWS = SEG * SEGS
REFS = 2 * SEGS
NB_DEV = 8
NB_LEN = 128
NB_BITS = 3
CAP = 2
PAIR = CAP * SEG
TAIL = 32
PART = NZ * DH + TAIL
MB = 1 << 20


def near_kernel(plan_ref, *refs):
    q_refs, kv_refs, (kv_ref, sem), rest = refs[:NY], refs[NY : NY + NZ + 1], refs[-2:], refs[NY + NZ + 1 : -2]
    zi = pl.program_id(0)
    half = NZ // 2

    @pl.when(zi == 0)
    def _():
        for r in range(NZ + 1):
            to = r if r <= half else r - 1
            dst = kv_ref.at[to]
            if r in (half, half + 1):
                dst = kv_ref.at[to, pl.ds(r - half, 1)]
            pltpu.make_async_copy(kv_refs[r], dst, sem.at[to]).start()

    pltpu.make_async_copy(kv_refs[0], kv_ref.at[zi], sem.at[zi]).wait()
    attn_kernel(True, plan_ref, *q_refs, kv_ref.at[zi], *rest)


def gathered_kernel(at, plan_ref, *refs):
    q_refs, source, (kv_ref, sem), rest = refs[:NY], refs[NY], refs[-2:], refs[NY + 1 : -2]
    zi = pl.program_id(0)

    @pl.when(zi == 0)
    def _():
        for r in range(NZ):
            pltpu.make_async_copy(source.at[r, at], kv_ref.at[r], sem.at[r]).start()

    pltpu.make_async_copy(source.at[zi, at], kv_ref.at[zi], sem.at[zi]).wait()
    attn_kernel(False, plan_ref, *q_refs, kv_ref.at[zi], *rest)


def attn_kernel(apart, plan_ref, *refs):
    q_refs, kv_ref, out_refs, lse_ref = refs[:NY], refs[NY], refs[NY + 1 : -1], refs[-1]
    zi = pl.program_id(0)
    yme = plan_ref[NZ * NY * CAP]
    place = (zi + plan_ref[NZ * NY * CAP + 1]) & (NZ - 1)
    if apart:
        outs = out_refs
    else:
        outs = [out_refs[0].at[(yme + a) & (NY - 1)] for a in range(NY)]
    low = lax.broadcasted_iota(jnp.int32, (1, PAIR), 1) < SEG
    nt = (((1,), (1,)), ((), ()))
    scores, values = [], []
    for a in range(NY):
        queries, keys = [], []
        for r in range(CAP):
            code = plan_ref[(zi * NY + a) * CAP + r]
            at = code & (NB_DEV - 1)
            start = pl.multiple_of((code >> NB_BITS) * SEG, SEG)
            queries.append(q_refs[a][pl.ds(start, SEG), :])
            keys.append(kv_ref[0, at])
            values.append(kv_ref[1, at])
        values[-2:] = [jnp.concatenate(values[-2:], axis=0)]
        pair = jnp.concatenate(queries, axis=0)
        keys = jnp.concatenate(keys, axis=0)
        both = lax.dot_general(keys, pair, nt, preferred_element_type=jnp.float32)
        scores.append(jnp.where(low, both[:NB_LEN], both[NB_LEN:]))
    scores = jnp.concatenate(scores, axis=1) * (DH**-0.5)
    top = jnp.max(scores, axis=0, keepdims=True)
    weights = jnp.exp(scores - top)
    total = jnp.sum(weights, axis=0, keepdims=True)
    rounded = weights.astype(jnp.bfloat16)
    inverse = 1.0 / total
    lse = top + jnp.log(total)
    hi = lse.astype(jnp.bfloat16).astype(jnp.float32)
    mid = (lse - hi).astype(jnp.bfloat16).astype(jnp.float32)
    lo = lse - hi - mid
    start = pl.multiple_of(place * DH, DH)
    for a in range(NY):
        at = slice(a * PAIR, (a + 1) * PAIR)
        both = jnp.dot(values[a], rounded[:, at], preferred_element_type=jnp.float32)
        out = (jnp.where(low, both[:DH], both[DH:]) * inverse[:, at]).astype(jnp.bfloat16)
        outs[a][pl.ds(start, DH), :] = out
        for k, piece in enumerate((hi, mid, lo)):
            lse_ref[a, pl.ds(k * NZ + place, 1), :] = piece[:, at]

    @pl.when(zi == NZ - 1)
    def _():
        for a in range(NY):
            lse_ref[a, 3 * NZ :, :] = jnp.zeros((TAIL - 3 * NZ, PAIR), jnp.float32)
            tail = lse_ref[a].astype(jnp.bfloat16)
            outs[a][NZ * DH :, :] = tail


def attend(plan, q_blocks, kv, head, at):
    near = isinstance(kv, list)
    scratch = [
        pltpu.VMEM((NY, TAIL, PAIR), jnp.float32),
        pltpu.VMEM((NZ, 2, NB_DEV, DH, DH), jnp.bfloat16),
        pltpu.SemaphoreType.DMA((NZ,)),
    ]
    if near:
        kernel, operands = near_kernel, kv
        kv_specs = [pl.BlockSpec(memory_space=pl.ANY)] * len(kv)
        out_specs = [pl.BlockSpec((PART, PAIR), lambda z, *_: (0, 0))] * NY
        out_shape = [jax.ShapeDtypeStruct((PART, PAIR), jnp.bfloat16)] * NY
    else:
        kernel, operands = functools.partial(gathered_kernel, at), [kv]
        kv_specs = [pl.BlockSpec(memory_space=pl.ANY)]
        out_specs = pl.BlockSpec((NY, PART, PAIR), lambda z, *_: (0, 0, 0))
        out_shape = jax.ShapeDtypeStruct((NY, PART, PAIR), jnp.bfloat16)
    return pl.pallas_call(
        kernel,
        grid_spec=pltpu.PrefetchScalarGridSpec(
            num_scalar_prefetch=1,
            grid=(NZ,),
            in_specs=[pl.BlockSpec((ROWS, DH), lambda z, *_: (0, head))] * NY + kv_specs,
            out_specs=out_specs,
            scratch_shapes=scratch,
        ),
        out_shape=out_shape,
        compiler_params=pltpu.CompilerParams(vmem_limit_bytes=60 * MB),
        cost_estimate=pl.CostEstimate(
            flops=32 * 4 * 2 * DH**3 * 4, bytes_accessed=20 * MB, transcendentals=32 * DH * DH
        ),
        name="attend",
    )(plan, *q_blocks, *operands)


def merge_kernel(counts, place_ref, *refs):
    part_refs, (out_ref, lse_ref, near_ref) = refs[: sum(counts)], refs[sum(counts) :]
    low = lax.broadcasted_iota(jnp.int32, (1, PAIR), 1) < SEG
    for head, count in enumerate(counts):
        head_refs, part_refs = part_refs[:count], part_refs[count:]
        if count > 1:
            part_ref = near_ref
            for y in range(NY):
                near_ref[y] = head_refs[y][...]
        else:
            part_ref = head_refs[0]
        for y in range(NY):
            tail = part_ref[y, NZ * DH :, :].astype(jnp.float32)
            lse_ref[y] = tail[0:NZ] + tail[NZ : 2 * NZ] + tail[2 * NZ : 3 * NZ]
        for p in range(SEGS // 2):
            sums, lses = [], []
            for j in range(2):
                halves_o, halves_l = [], []
                for side in range(2):
                    code = place_ref[2 * (2 * p + side) + j + (REFS if count > 1 else 0)]
                    half, y, z = code & 1, (code >> 1) & (NY - 1), code >> 3
                    start = pl.multiple_of(z * DH, DH)
                    part = part_ref[y, pl.ds(start, DH), :].astype(jnp.float32)
                    lse = lse_ref[y, pl.ds(z, 1), :]
                    shift = jnp.where(half == side, 0, SEG)
                    halves_o.append(pltpu.roll(part, shift, 1))
                    halves_l.append(pltpu.roll(lse, shift, 1))
                sums.append(jnp.where(low, halves_o[0], halves_o[1]))
                lses.append(jnp.where(low, halves_l[0], halves_l[1]))
            top = jnp.maximum(lses[0], lses[1])
            f0, f1 = jnp.exp(lses[0] - top), jnp.exp(lses[1] - top)
            scale = 1.0 / (f0 + f1)
            context = (f0 * scale) * sums[0] + (f1 * scale) * sums[1]
            out_ref[p * PAIR : (p + 1) * PAIR, head * DH : (head + 1) * DH] = jnp.transpose(
                context
            ).astype(jnp.bfloat16)


def merge(place, *heads):
    counts = [len(parts) for parts in heads]
    near_shape = (NY, PART, PAIR) if max(counts) > 1 else (1, 16, PAIR)
    return pl.pallas_call(
        functools.partial(merge_kernel, counts),
        grid_spec=pltpu.PrefetchScalarGridSpec(
            num_scalar_prefetch=1,
            grid=(),
            in_specs=[pl.BlockSpec(memory_space=pltpu.VMEM)] * sum(counts),
            out_specs=pl.BlockSpec(memory_space=pltpu.VMEM),
            scratch_shapes=[
                pltpu.VMEM((NY, NZ, PAIR), jnp.float32),
                pltpu.VMEM(near_shape, jnp.bfloat16),
            ],
        ),
        out_shape=jax.ShapeDtypeStruct((ROWS, len(heads) * DH), jnp.bfloat16),
        compiler_params=pltpu.CompilerParams(vmem_limit_bytes=16 * MB),
        cost_estimate=pl.CostEstimate(
            flops=8 * DH * ROWS, bytes_accessed=8 * MB, transcendentals=2 * ROWS
        ),
        name="merge",
    )(place, *[part for parts in heads for part in parts])


def project(where, spread, shares, other, total, last):
    cols = other.shape[2]
    width = 512
    first = total is None
    sq = pl.Squeezed()
    groups = len(spread) * NX * NC

    def kernel(_, *refs):
        ctx, wgt = refs[:groups], refs[groups : 2 * groups]
        out_ref = refs[-1]
        left = jnp.concatenate([ref[...] for ref in ctx], axis=1)
        right = jnp.concatenate([ref[...] for ref in wgt], axis=0)
        term = jnp.dot(left, right, preferred_element_type=jnp.float32)
        if not first:
            term = term + refs[2 * groups][...]
        out_ref[...] = term.astype(out_ref.dtype)

    def own_rows(head, d):
        at_x = (lambda at: at[0] * NC) if d == 0 else (lambda at: 0)
        return lambda n, at: (head, (at_x(at) + at[1]) * (cols // width) + n)

    def other_rows(head, d):
        return lambda n, *_: (d, head, n)

    block = pl.BlockSpec((ROWS, width), lambda n, *_: (0, n))
    in_specs = [pl.BlockSpec((ROWS, DH), lambda n, *_: (0, 0))] * groups
    operands = [context for _, contexts in spread for context in contexts]
    for head, _ in spread:
        for d in range(NX):
            in_specs += [
                pl.BlockSpec((DH, width), own_rows(head, d)),
                pl.BlockSpec((sq, DH, width), other_rows(head, d)),
            ]
            operands += [shares[d], other]
    if not first:
        in_specs.append(block)
        operands.append(total)
    return pl.pallas_call(
        kernel,
        grid_spec=pltpu.PrefetchScalarGridSpec(
            num_scalar_prefetch=1, grid=(cols // width,), in_specs=in_specs, out_specs=block
        ),
        out_shape=jax.ShapeDtypeStruct((ROWS, cols), jnp.bfloat16),
        input_output_aliases={} if first or last else {2 * groups + 1: 0},
        compiler_params=pltpu.CompilerParams(vmem_limit_bytes=60 * MB),
        cost_estimate=pl.CostEstimate(
            flops=2 * ROWS * cols * groups * DH, bytes_accessed=12 * MB, transcendentals=0
        ),
        name="project",
    )(where, *operands)


def ring(axis, size, step):
    return [(i, (i + step) % size) for i in range(size)]


def earlier_equal(keys):
    order = jnp.arange(keys.shape[-1])
    same = keys[..., :, None] == keys[..., None, :]
    return jnp.sum((same & (order[None, :] < order[:, None])).astype(jnp.int32), axis=-1)


def body(queries, neighbour_ids, neighbour_kv, out_weight):
    heads = queries.shape[1] // DH
    zme, yme, xme, cme = (lax.axis_index(a).astype(jnp.int32) for a in ("z", "y", "x", "core"))
    cols = out_weight.shape[1] // (NX * NC)
    barrier = lax.optimization_barrier

    def after(value, *others):
        return barrier((value, others))[0]

    block = neighbour_kv.reshape(NB_DEV, NB_LEN, 2, heads, DH)
    keys = jnp.transpose(block[:, :, 0], (2, 0, 1, 3))
    values = jnp.transpose(block[:, :, 1], (2, 0, 3, 1))
    own = jnp.stack([keys, values], axis=1)
    kv_mid = lax.all_gather(own[1:3], "z")
    kv_last = lax.all_gather(own[3:], "z")

    def up(value):
        return lax.ppermute(value, "z", ring("z", NZ, 1))

    def down(value):
        return lax.ppermute(value, "z", ring("z", NZ, -1))

    below, above = [own[0]], [own[0]]
    for _ in range(NZ // 2 - 1):
        below.append(up(below[-1]))
        above.append(down(above[-1]))
    kv_near = above + [up(below[-1][:1]), down(above[-1][1:])] + below[:0:-1]

    chip_cols = NC * cols
    shares = [out_weight]
    for d in range(1, NX):
        target = (xme + d) % NX
        share = lax.dynamic_slice_in_dim(out_weight, target * chip_cols, chip_cols, 1)
        shares.append(lax.ppermute(share, "x", ring("x", NX, d)))

    ids = neighbour_ids.reshape(-1)
    width = queries.shape[1]
    id_rows = jnp.pad(ids.astype(queries.dtype).reshape(1, REFS), ((0, 15), (0, width - REFS)))
    asker = jnp.concatenate([queries, id_rows], axis=0)
    q_all = [asker] + [lax.ppermute(asker, "y", ring("y", NY, -d)) for d in range(1, NY)]
    asked = jnp.stack([q[ROWS, :REFS] for q in q_all]).astype(jnp.int32)

    holder = asked >> NB_BITS
    rank = earlier_equal(holder)
    want = (jnp.arange(NZ) * NY + yme)[:, None, None, None]
    hit = (holder[None, :, None, :] == want) & (
        rank[None, :, None, :] == jnp.arange(CAP)[None, None, :, None]
    )
    code = (jnp.arange(REFS) // 2) * NB_DEV + (asked & (NB_DEV - 1))
    plan = jnp.sum(jnp.where(hit, code[None, :, None, :], 0), axis=-1)
    plan_near = jnp.concatenate([jnp.roll(plan, -zme, axis=0).reshape(-1), yme[None], zme[None]])
    plan = jnp.concatenate([plan.reshape(-1), yme[None], jnp.zeros((1,), jnp.int32)])
    mine = ids >> NB_BITS
    near_mine = (mine // NY) * NY + ((yme - mine) & (NY - 1))
    place = jnp.concatenate([mine, near_mine]) * CAP + jnp.tile(earlier_equal(mine), 2)

    swap = [(0, 1), (1, 0)]

    def near(context):
        return [context] + [lax.ppermute(context, "x", ring("x", NX, d)) for d in range(1, NX)]

    def both_cores(came):
        return [c for own in came for c in (own, lax.ppermute(own, "core", swap))]

    def send(parts):
        return lax.all_to_all(parts, "y", 0, 0, tiled=True)

    parts0 = attend(plan_near, q_all, kv_near, 0, 0)
    back0 = [lax.ppermute(p, "y", ring("y", NY, d)) if d else p for d, p in enumerate(parts0)]
    came0 = near(merge(place, back0))

    parts1 = attend(plan, q_all, after(kv_mid, back0), 1, 0)
    back1 = send(parts1)
    parts2 = attend(plan, q_all, kv_mid, 2, 1)

    shares = after(after(shares, back0), parts1)
    first_col = [xme * chip_cols] + [0] * (NX - 1)
    rest = [
        lax.dynamic_slice_in_dim(share, at + (1 - cme) * cols, cols, 1)
        for share, at in zip(shares, first_col)
    ]
    other = lax.ppermute(jnp.stack(rest), "core", swap)
    where = jnp.stack([xme, cme])

    back2 = send(after(parts2, came0))
    context1 = merge(place, [after(back1, parts2)])
    came1 = near(context1)
    parts3 = attend(plan, q_all, after(kv_last, context1), 3, 0)
    back3 = send(after(parts3, came1))
    context2 = merge(place, [after(back2, parts3)])
    came2 = near(context2)
    spread = [(0, both_cores(after(came0, context2))), (1, both_cores(came1))]
    total = project(where, spread, shares, other, None, False)
    context3 = merge(place, [after(back3, total)])
    came3 = near(after(context3, came2))
    spread = [(2, both_cores(after(came2, context3)))]
    total = project(where, spread, shares, other, total, False)
    came3[1:] = after(came3[1:], total)
    return project(where, [(3, both_cores(came3))], shares, other, total, True)


def solution(mesh):
    fine = Mesh(np.asarray(mesh.devices).reshape(NZ, NY, NX, NC), ("z", "y", "x", "core"))
    store, head = ("z", "y"), ("x", "core")
    in_specs = (
        P(store, head),
        P(store, None),
        P(store, None, None, head),
        P(head, None),
    )
    return jax.shard_map(
        body, mesh=fine, in_specs=in_specs, out_specs=P(store, head), check_vma=False
    )
```
